32 devices in a mesh: dp: 8 (over y, x, core), fsdp: 4 (over z).
Axes of the slice: x: 2, y: 2, z: 4, core: 2. Of those that a mesh axis runs over, the one named last changes fastest.
Arguments:
- grad_partials: bfloat16 [8, 4, 2, 16, 5120], P('dp', 'fsdp'), may hold values from -5 to 5
- momentum: float32 [8, 2, 16, 5120], P('dp', None, 'fsdp'), may hold values from -6 to 6
- params: float32 [2, 16, 5120], P(None, 'fsdp'), may hold values from -6 to 6
- kept: int32 [8], replicated, may hold values from 0 to 63, as said below
Outputs:
- new_params: float32 [2, 16, 5120], P(None, 'fsdp')
- new_momentum: float32 [8, 2, 16, 5120], P('dp', None, 'fsdp')
The draws below stay inside these ranges and needn't reach their ends.
Inputs may be any that keep to these rules, and one draw needn't show every extreme that they name: `kept`: 8 distinct coefficient indices.
All inputs are finite; a program needn't handle non-finite values.
Results may differ from the reference program's by a relative error of at most 0.0003.
Values sent between devices are 32-bit elements; how exact they have to be, the bound alone decides.
A program may use at most 64 MiB of HBM per device.

```python
import jax
import jax.numpy as jnp
from jax import lax

SPAN = 64
KEEP = 8
ROW_VALS = 5120
LAYERS = 2
ROWS = 16
N_DP = 8
N_FSDP = 4


def draw_kept(key, part):
    key = jax.random.fold_in(key, 7)
    inner_key = jax.random.fold_in(key, 1)
    order_key = jax.random.fold_in(key, 2)
    inner = jax.random.permutation(inner_key, SPAN - 2)[:KEEP - 2].astype(jnp.int32) + 1
    ends = jnp.array([0, SPAN - 1], dtype=jnp.int32)
    joined = jnp.concatenate([ends, inner])
    return jax.random.permutation(order_key, joined).astype(jnp.int32)


def raised(values, own_key, source, target, blocks, factor):
    def block_of(dim):
        return (jnp.arange(values.shape[dim]) // (values.shape[dim] // blocks)).reshape((-1,) + (1,) * (values.ndim - 1 - dim))

    near = jax.random.permutation(own_key, blocks)[block_of(target)]
    second = (block_of(target) + blocks // 2) % blocks
    return jnp.where((block_of(source) == near) | (block_of(source) == second), factor * values, values)


def shard_levels(own_key, dims, pieces, least, high):
    def one(axis_at, blocks):
        steps = jax.random.uniform(jax.random.fold_in(jax.random.fold_in(own_key, 6), axis_at), (blocks,), jnp.float32, least / len(pieces), high / len(pieces))
        return jnp.repeat(jnp.exp(steps), dims[axis_at] // blocks).reshape((-1,) + (1,) * (len(dims) - axis_at - 1))

    factor_of = one(*pieces[0])
    for cut in pieces[1:]:
        factor_of = factor_of * one(*cut)
    return factor_of


def gaussian(own_key, dims, scale, bound, cuts=(), kind=jnp.bfloat16):
    result = jax.random.normal(own_key, dims, jnp.float32) * scale
    if len(cuts) > 0:
        result = shard_levels(own_key, dims, cuts, -0.22, 0.18) * result
    return jnp.clip(result, min=-bound, max=bound).astype(kind)


def noise_with(key, extent, deviation, most, split, heavy, kind=jnp.bfloat16):
    values = deviation * jax.random.normal(key, extent, jnp.float32)
    if split:
        values = values * shard_levels(key, extent, split, -0.22, 0.18)
    return jnp.clip(raised(values, jax.random.fold_in(key, 3), *heavy), -most, most).astype(kind)


def setup_inputs(seed: int = 0) -> dict:
    key_list = jax.random.split(jax.random.key(seed), 5)
    grad_partials = noise_with(key_list[0], (N_DP, N_FSDP, LAYERS, ROWS, ROW_VALS), 0.25, 5.0, ((0, 8), (1, 4)), (1, 3, 4, 2.0))
    momentum = gaussian(key_list[1], (N_DP, LAYERS, ROWS, ROW_VALS), 1.0, 6.0, ((0, 8), (2, 4)), jnp.float32)
    params = gaussian(key_list[2], (LAYERS, ROWS, ROW_VALS), 1.0, 6.0, ((1, 4),), jnp.float32)
    kept = draw_kept(jax.random.fold_in(key_list[4], 71), 0)
    return {"grad_partials": grad_partials, "momentum": momentum, "params": params, "kept": kept}


def dct_table():
    k = lax.broadcasted_iota(jnp.float32, (SPAN, SPAN), 0)
    n = lax.broadcasted_iota(jnp.float32, (SPAN, SPAN), 1)
    scale = jnp.where(k == 0, jnp.sqrt(1.0 / SPAN), jnp.sqrt(2.0 / SPAN))
    return scale * jnp.cos(jnp.pi * (2.0 * n + 1.0) * k / (2.0 * SPAN))

def picked_rows(kept):
    onehot = (kept[:, None] == jnp.arange(SPAN, dtype=jnp.int32)[None, :]).astype(jnp.float32)
    return jnp.dot(onehot, dct_table(), precision=lax.Precision.HIGHEST)

def reference(grad_partials, momentum, params, kept):
    picked = picked_rows(kept)
    blocks = ROW_VALS // SPAN

    def one_replica(pair):
        parts, state = pair
        grad = lax.optimization_barrier(jnp.sum(parts.astype(jnp.float32), axis=0))
        moment = 0.9 * state + grad
        spans = moment.reshape(LAYERS, ROWS, blocks, SPAN)
        coeffs = jnp.einsum('lrcn,jn->lrcj', spans, picked, precision=lax.Precision.HIGHEST)
        local = jnp.einsum('lrcj,jn->lrcn', coeffs, picked, precision=lax.Precision.HIGHEST)
        return (moment - local.reshape(moment.shape), coeffs.reshape(LAYERS, ROWS, blocks * KEEP))
    new_momentum, coeffs = lax.map(one_replica, (grad_partials, momentum))
    shared = lax.optimization_barrier(jnp.sum(coeffs, axis=0)) / N_DP
    update = jnp.einsum('lrcj,jn->lrcn', shared.reshape(LAYERS, ROWS, blocks, KEEP), picked, precision=lax.Precision.HIGHEST)
    new_params = params - update.reshape(params.shape)
    return (new_params, new_momentum)
```

```python
import functools
import math

import jax
import jax.numpy as jnp
from jax import lax
from jax.experimental import pallas as pl
from jax.experimental.pallas import tpu as pltpu
from jax.sharding import PartitionSpec as P

SPAN = 64
KEEP = 8
PIECE = 1024
GROUP = 256
LAG = 2
F32 = jnp.float32
BF16 = jnp.bfloat16


def cosine_rows(k, n):
    turn = ((2 * n + 1) * k) & (4 * SPAN - 1)
    turn = jnp.minimum(turn, 4 * SPAN - turn)
    scale = jnp.where(k == 0, math.sqrt(1.0 / SPAN), math.sqrt(2.0 / SPAN)).astype(F32)
    return scale * jnp.cos(turn.astype(F32) * (math.pi / (2 * SPAN)))


def halves(x):
    high = x.astype(BF16)
    return high, (x - high.astype(F32)).astype(BF16)


def dot(a, b):
    return jnp.dot(a, b, preferred_element_type=F32)


def kernel(
    n_dp, n_fsdp, batches,
    grad_hbm, mom_hbm, par_hbm, kept_ref, new_par_hbm, new_mom_hbm,
    grad, mom, par, mine, inbox, coeffs, w_coef, w_proj, w_back, new_par, new_mom,
    load_sem, store_sem, send_sem, recv_sem, dp_send, dp_recv,
):
    layers, rows, cols = grad.shape
    own = rows // n_fsdp
    pieces = cols // PIECE
    dp, me = lax.axis_index("dp"), lax.axis_index("fsdp")

    loads = [
        pltpu.make_async_copy(grad_hbm.at[0, 0], grad, load_sem.at[0]),
        pltpu.make_async_copy(mom_hbm.at[0], mom, load_sem.at[1]),
        pltpu.make_async_copy(par_hbm, par, load_sem.at[2]),
    ]
    for load in loads:
        load.start()

    barrier = pltpu.get_barrier_semaphore()
    for i in range(1, n_dp):
        pl.semaphore_signal(
            barrier, inc=1, device_id={"dp": lax.rem(dp + i, n_dp)}, device_id_type=pl.DeviceIdType.MESH
        )

    near = me // (n_fsdp // 2)
    far = 1 - near
    near_pos = near * (n_fsdp - 1 - me) + far * me
    far_pos = n_fsdp - 1 - near_pos
    near_next, far_next = me + 1 - 2 * near, me + 1 - 2 * far
    pl.semaphore_signal(barrier, inc=1, device_id={"fsdp": near_next}, device_id_type=pl.DeviceIdType.MESH)

    @pl.when(near_pos > 0)
    def _():
        pl.semaphore_signal(barrier, inc=1, device_id={"fsdp": far_next}, device_id_type=pl.DeviceIdType.MESH)

    loads[0].wait()
    for layer in range(layers):
        for p in range(pieces):
            at = pl.ds(p * PIECE, PIECE)
            x = grad[layer, :, at].astype(F32)
            for d in range(n_fsdp):
                mine[d, layer * own:(layer + 1) * own, at] = x[d * own:(d + 1) * own]

    pl.semaphore_wait(barrier, n_dp + (near_pos > 0).astype(jnp.int32))

    def forward(flow, q, p):
        at = pl.ds(p * PIECE, PIECE)
        d = flow * (n_fsdp - 1 - q) + (1 - flow) * q
        return pltpu.make_async_remote_copy(
            src_ref=mine.at[d, :, at], dst_ref=inbox.at[flow, d, :, at],
            send_sem=send_sem.at[flow, q, p], recv_sem=recv_sem.at[flow, q, p],
            device_id={"fsdp": me + 1 - 2 * flow}, device_id_type=pl.DeviceIdType.MESH,
        )

    def add(flow, q, p):
        at = pl.ds(p * PIECE, PIECE)
        d = flow * (n_fsdp - 1 - q) + (1 - flow) * q
        forward(flow, q, p).wait_recv()
        mine[d, :, at] += inbox[flow, d, :, at]

    near_list = [(q, p) for q in range(n_fsdp - 1, 0, -1) for p in range(pieces)]
    far_list = [(q, p) for q in range(n_fsdp - 1, n_fsdp // 2, -1) for p in range(pieces)]

    @pl.when(near_pos == 0)
    def _():
        for q, p in near_list:
            forward(near, q, p).start()

    def by_index(shape, dim):
        j = lax.broadcasted_iota(jnp.int32, shape, dim) % KEEP
        k = jnp.zeros(shape, jnp.int32)
        for i in range(KEEP):
            k = jnp.where(j == i, kept_ref[i], k)
        return k

    lanes = 128
    row = cosine_rows(by_index((KEEP, lanes), 0), lax.broadcasted_iota(jnp.int32, (KEEP, lanes), 1) % SPAN)
    column = cosine_rows(by_index((SPAN, lanes), 1), lax.broadcasted_iota(jnp.int32, (SPAN, lanes), 0))
    lane_block = lax.broadcasted_iota(jnp.int32, (SPAN, lanes), 1) // KEEP
    coef = jnp.concatenate([jnp.where(lane_block == b, column, 0.0) for b in range(GROUP // SPAN)], axis=0)
    wide = jnp.concatenate([row] * (PIECE // lanes), axis=1)
    wide_block = lax.broadcasted_iota(jnp.int32, (KEEP, PIECE), 1) // SPAN
    back = jnp.concatenate([jnp.where(wide_block == b, wide, 0.0) for b in range(PIECE // SPAN)], axis=0)
    high, low = halves(coef)
    w_coef[:, :lanes] = high
    w_coef[:, lanes:] = low
    high, low = halves(back)
    w_back[:lanes] = high
    w_back[lanes:] = low
    proj = jnp.dot(coef, back[:, :GROUP], precision=lax.Precision.HIGHEST, preferred_element_type=F32)
    high, low = halves(proj)
    w_proj[:, :GROUP] = high
    w_proj[:, GROUP:] = low

    def near_step(q, p):
        @pl.when((near_pos > 0) & (near_pos < q))
        def _():
            add(near, q, p)
            forward(near, q, p).start()

    def far_step(q, p):
        @pl.when(far_pos < q)
        def _():
            add(far, q, p)
            forward(far, q, p).start()

    for i in range(len(near_list)):
        if near_list[i][0] > 1:
            near_step(*near_list[i])
        if 0 <= i - LAG < len(far_list):
            far_step(*far_list[i - LAG])

    def dp_copy(i, batch):
        at = pl.ds(batch[0], batch[1] - batch[0])
        b = batches.index(batch)
        return pltpu.make_async_remote_copy(
            src_ref=coeffs.at[dp, at], dst_ref=coeffs.at[dp, at],
            send_sem=dp_send.at[i, b], recv_sem=dp_recv.at[i, b],
            device_id={"dp": lax.rem(dp + i, n_dp)}, device_id_type=pl.DeviceIdType.MESH,
        )

    def dp_arrival(i, batch):
        at = pl.ds(batch[0], batch[1] - batch[0])
        b = batches.index(batch)
        source = lax.rem(dp + n_dp - i, n_dp)
        return pltpu.make_async_remote_copy(
            src_ref=coeffs.at[source, at], dst_ref=coeffs.at[source, at],
            send_sem=dp_send.at[i, b], recv_sem=dp_recv.at[i, b],
            device_id={"dp": lax.rem(dp + i, n_dp)}, device_id_type=pl.DeviceIdType.MESH,
        )

    loads[1].wait()
    parts = PIECE // GROUP
    for batch in batches:
        kept_parts = []
        for p in range(*batch):
            at = pl.ds(p * PIECE, PIECE)
            add(far, far_pos, p)

            @pl.when(near_pos > 0)
            def _():
                add(near, near_pos, p)

            old = jnp.concatenate([mom[layer, :, at] for layer in range(layers)], axis=0)
            moment = 0.9 * old + mine[me, :, at]
            height = moment.shape[0]
            tall = jnp.concatenate([moment[:, q * GROUP:(q + 1) * GROUP] for q in range(parts)], axis=0)
            both = jnp.concatenate(halves(tall), axis=0)
            out = dot(both, w_coef[...])
            out = out[:parts * height] + out[parts * height:]
            out = out[:, :lanes] + out[:, lanes:]
            packed = out[:height]
            for q in range(1, parts):
                packed += pltpu.roll(out[q * height:(q + 1) * height], q * (lanes // parts), 1)
            coeffs[dp, p] = packed
            kept_parts.append((p, tall, both))
        for i in range(1, n_dp):
            dp_copy(i, batch).start()
        for p, tall, both in kept_parts:
            half = tall.shape[0]
            out = dot(both, w_proj[...])
            local = out[:half, :GROUP] + (out[half:, :GROUP] + out[:half, GROUP:])
            rest = tall - local
            height = half // parts
            for q in range(parts):
                at = pl.ds(p * PIECE + q * GROUP, GROUP)
                for layer in range(layers):
                    new_mom[layer, :, at] = rest[q * height + layer * own:q * height + (layer + 1) * own]
    store_mom = pltpu.make_async_copy(new_mom, new_mom_hbm.at[0], store_sem.at[0])
    store_mom.start()

    loads[2].wait()
    for batch in batches:
        for i in range(1, n_dp):
            dp_arrival(i, batch).wait_recv()
        for p in range(*batch):
            at = pl.ds(p * PIECE, PIECE)
            total = coeffs[0, p]
            for r in range(1, n_dp):
                total += coeffs[r, p]
            high, low = halves(total * (1.0 / n_dp) if n_dp & (n_dp - 1) == 0 else total / n_dp)
            height = high.shape[0]
            left = jnp.concatenate([high, low], axis=0)
            right = jnp.concatenate([high, jnp.zeros_like(low)], axis=0)
            out = dot(jnp.concatenate([left, right], axis=1), w_back[...])
            update = out[:height] + out[height:]
            for layer in range(layers):
                new_par[layer, :, at] = par[layer, :, at] - update[layer * own:(layer + 1) * own]
    store_par = pltpu.make_async_copy(new_par, new_par_hbm, store_sem.at[1])
    store_par.start()

    for q, p in near_list:
        @pl.when(near_pos < q)
        def _():
            forward(near, q, p).wait_send()

    for q, p in far_list:
        @pl.when(far_pos < q)
        def _():
            forward(far, q, p).wait_send()

    for batch in batches:
        for i in range(1, n_dp):
            dp_copy(i, batch).wait_send()
    store_mom.wait()
    store_par.wait()


def shards(n_dp, n_fsdp, grad_partials, momentum, params, kept):
    _, _, layers, rows, cols = grad_partials.shape
    own = rows // n_fsdp
    pieces = cols // PIECE
    batches = ((0, pieces // 2), (pieces // 2, pieces - 1), (pieces - 1, pieces))
    held = (layers, own, cols)
    chunk = (n_fsdp, layers * own, cols)
    anywhere = pl.BlockSpec(memory_space=pl.ANY)
    sem = pltpu.SemaphoreType.DMA
    return pl.pallas_call(
        functools.partial(kernel, n_dp, n_fsdp, batches),
        out_shape=(
            jax.ShapeDtypeStruct(params.shape, F32),
            jax.ShapeDtypeStruct(momentum.shape, F32),
        ),
        in_specs=[anywhere, anywhere, anywhere, pl.BlockSpec(memory_space=pltpu.SMEM)],
        out_specs=(anywhere, anywhere),
        scratch_shapes=[
            pltpu.VMEM((layers, rows, cols), BF16),
            pltpu.VMEM(held, F32),
            pltpu.VMEM(held, F32),
            pltpu.VMEM(chunk, F32),
            pltpu.VMEM((2,) + chunk, F32),
            pltpu.VMEM((n_dp, pieces, layers * own, 128), F32),
            pltpu.VMEM((GROUP, 256), BF16),
            pltpu.VMEM((GROUP, 2 * GROUP), BF16),
            pltpu.VMEM((256, PIECE), BF16),
            pltpu.VMEM(held, F32),
            pltpu.VMEM(held, F32),
            sem((3,)),
            sem((2,)),
            sem((2, n_fsdp, pieces)),
            sem((2, n_fsdp, pieces)),
            sem((n_dp, len(batches))),
            sem((n_dp, len(batches))),
        ],
        compiler_params=pltpu.CompilerParams(
            collective_id=0, has_side_effects=True, vmem_limit_bytes=60 * 1024 * 1024
        ),
    )(grad_partials, momentum, params, kept)


def solution(mesh):
    placed = (
        P("dp", "fsdp", None, None, None),
        P("dp", None, "fsdp", None),
        P(None, "fsdp", None),
        P(),
    )
    return jax.shard_map(
        functools.partial(shards, mesh.shape["dp"], mesh.shape["fsdp"]),
        mesh=mesh,
        in_specs=placed,
        out_specs=(P(None, "fsdp", None), P("dp", None, "fsdp", None)),
        check_vma=False,
    )
```

```python
import functools
import math

import jax
import jax.numpy as jnp
from jax import lax
from jax.experimental import pallas as pl
from jax.experimental.pallas import tpu as pltpu
from jax.sharding import PartitionSpec as P

SPAN = 64
KEEP = 8
PIECE = 1024
GROUP = 256
LAG = 2
F32 = jnp.float32
BF16 = jnp.bfloat16


def cosine_rows(k, n):
    turn = ((2 * n + 1) * k) & (4 * SPAN - 1)
    turn = jnp.minimum(turn, 4 * SPAN - turn)
    scale = jnp.where(k == 0, math.sqrt(1.0 / SPAN), math.sqrt(2.0 / SPAN)).astype(F32)
    return scale * jnp.cos(turn.astype(F32) * (math.pi / (2 * SPAN)))


def halves(x):
    high = x.astype(BF16)
    return high, (x - high.astype(F32)).astype(BF16)


def dot(a, b):
    return jnp.dot(a, b, preferred_element_type=F32)


def kernel(
    n_dp, n_fsdp, batches,
    grad_hbm, mom_hbm, par_hbm, kept_hbm, new_par, new_mom,
    kept_ref, grad, mom, par, mine, inbox, coeffs, w_coef, w_proj, w_back,
    load_sem, send_sem, recv_sem, dp_send, dp_recv,
):
    layers, rows, cols = grad.shape
    own = rows // n_fsdp
    pieces = cols // PIECE
    dp, me = lax.axis_index("dp"), lax.axis_index("fsdp")

    loads = [
        pltpu.make_async_copy(grad_hbm.at[0, 0], grad, load_sem.at[0]),
        pltpu.make_async_copy(mom_hbm.at[0], mom, load_sem.at[1]),
        pltpu.make_async_copy(par_hbm, par, load_sem.at[2]),
        pltpu.make_async_copy(kept_hbm, kept_ref, load_sem.at[3]),
    ]
    for load in loads:
        load.start()

    barrier = pltpu.get_barrier_semaphore()
    for i in range(1, n_dp):
        pl.semaphore_signal(
            barrier, inc=1, device_id={"dp": lax.rem(dp + i, n_dp)}, device_id_type=pl.DeviceIdType.MESH
        )

    near = me // (n_fsdp // 2)
    far = 1 - near
    near_pos = near * (n_fsdp - 1 - me) + far * me
    far_pos = n_fsdp - 1 - near_pos
    near_next, far_next = me + 1 - 2 * near, me + 1 - 2 * far
    pl.semaphore_signal(barrier, inc=1, device_id={"fsdp": near_next}, device_id_type=pl.DeviceIdType.MESH)

    @pl.when(near_pos > 0)
    def _():
        pl.semaphore_signal(barrier, inc=1, device_id={"fsdp": far_next}, device_id_type=pl.DeviceIdType.MESH)

    loads[0].wait()
    for layer in range(layers):
        for p in range(pieces):
            at = pl.ds(p * PIECE, PIECE)
            x = grad[layer, :, at].astype(F32)
            for d in range(n_fsdp):
                mine[d, layer * own:(layer + 1) * own, at] = x[d * own:(d + 1) * own]

    pl.semaphore_wait(barrier, n_dp + (near_pos > 0).astype(jnp.int32))

    def forward(flow, q, p):
        at = pl.ds(p * PIECE, PIECE)
        d = flow * (n_fsdp - 1 - q) + (1 - flow) * q
        return pltpu.make_async_remote_copy(
            src_ref=mine.at[d, :, at], dst_ref=inbox.at[flow, d, :, at],
            send_sem=send_sem.at[flow, q, p], recv_sem=recv_sem.at[flow, q, p],
            device_id={"fsdp": me + 1 - 2 * flow}, device_id_type=pl.DeviceIdType.MESH,
        )

    def add(flow, q, p):
        at = pl.ds(p * PIECE, PIECE)
        d = flow * (n_fsdp - 1 - q) + (1 - flow) * q
        forward(flow, q, p).wait_recv()
        mine[d, :, at] += inbox[flow, d, :, at]

    near_list = [(q, p) for q in range(n_fsdp - 1, 0, -1) for p in range(pieces)]
    far_list = [(q, p) for q in range(n_fsdp - 1, n_fsdp // 2, -1) for p in range(pieces)]

    @pl.when(near_pos == 0)
    def _():
        for q, p in near_list:
            forward(near, q, p).start()

    loads[3].wait()

    def by_index(shape, dim):
        j = lax.broadcasted_iota(jnp.int32, shape, dim) % KEEP
        k = jnp.zeros(shape, jnp.int32)
        for i in range(KEEP):
            k = jnp.where(j == i, kept_ref[i], k)
        return k

    lanes = 128
    row = cosine_rows(by_index((KEEP, lanes), 0), lax.broadcasted_iota(jnp.int32, (KEEP, lanes), 1) % SPAN)
    column = cosine_rows(by_index((SPAN, lanes), 1), lax.broadcasted_iota(jnp.int32, (SPAN, lanes), 0))
    lane_block = lax.broadcasted_iota(jnp.int32, (SPAN, lanes), 1) // KEEP
    coef = jnp.concatenate([jnp.where(lane_block == b, column, 0.0) for b in range(GROUP // SPAN)], axis=0)
    wide = jnp.concatenate([row] * (PIECE // lanes), axis=1)
    wide_block = lax.broadcasted_iota(jnp.int32, (KEEP, PIECE), 1) // SPAN
    back = jnp.concatenate([jnp.where(wide_block == b, wide, 0.0) for b in range(PIECE // SPAN)], axis=0)
    high, low = halves(coef)
    w_coef[:, :lanes] = high
    w_coef[:, lanes:] = low
    high, low = halves(back)
    w_back[:lanes] = high
    w_back[lanes:] = low
    proj = jnp.dot(coef, back[:, :GROUP], precision=lax.Precision.HIGHEST, preferred_element_type=F32)
    high, low = halves(proj)
    w_proj[:, :GROUP] = high
    w_proj[:, GROUP:] = low

    def near_step(q, p):
        @pl.when((near_pos > 0) & (near_pos < q))
        def _():
            add(near, q, p)
            forward(near, q, p).start()

    def far_step(q, p):
        @pl.when(far_pos < q)
        def _():
            add(far, q, p)
            forward(far, q, p).start()

    for i in range(len(near_list)):
        if near_list[i][0] > 1:
            near_step(*near_list[i])
        if 0 <= i - LAG < len(far_list):
            far_step(*far_list[i - LAG])

    def dp_copy(i, batch):
        at = pl.ds(batch[0], batch[1] - batch[0])
        b = batches.index(batch)
        return pltpu.make_async_remote_copy(
            src_ref=coeffs.at[dp, at], dst_ref=coeffs.at[dp, at],
            send_sem=dp_send.at[i, b], recv_sem=dp_recv.at[i, b],
            device_id={"dp": lax.rem(dp + i, n_dp)}, device_id_type=pl.DeviceIdType.MESH,
        )

    def dp_arrival(i, batch):
        at = pl.ds(batch[0], batch[1] - batch[0])
        b = batches.index(batch)
        source = lax.rem(dp + n_dp - i, n_dp)
        return pltpu.make_async_remote_copy(
            src_ref=coeffs.at[source, at], dst_ref=coeffs.at[source, at],
            send_sem=dp_send.at[i, b], recv_sem=dp_recv.at[i, b],
            device_id={"dp": lax.rem(dp + i, n_dp)}, device_id_type=pl.DeviceIdType.MESH,
        )

    loads[1].wait()
    parts = PIECE // GROUP
    for batch in batches:
        kept_parts = []
        for p in range(*batch):
            at = pl.ds(p * PIECE, PIECE)
            add(far, far_pos, p)

            @pl.when(near_pos > 0)
            def _():
                add(near, near_pos, p)

            old = jnp.concatenate([mom[layer, :, at] for layer in range(layers)], axis=0)
            moment = 0.9 * old + mine[me, :, at]
            height = moment.shape[0]
            tall = jnp.concatenate([moment[:, q * GROUP:(q + 1) * GROUP] for q in range(parts)], axis=0)
            both = jnp.concatenate(halves(tall), axis=0)
            out = dot(both, w_coef[...])
            out = out[:parts * height] + out[parts * height:]
            out = out[:, :lanes] + out[:, lanes:]
            packed = out[:height]
            for q in range(1, parts):
                packed += pltpu.roll(out[q * height:(q + 1) * height], q * (lanes // parts), 1)
            coeffs[dp, p] = packed
            kept_parts.append((p, tall, both))
        for i in range(1, n_dp):
            dp_copy(i, batch).start()
        for p, tall, both in kept_parts:
            half = tall.shape[0]
            out = dot(both, w_proj[...])
            local = out[:half, :GROUP] + (out[half:, :GROUP] + out[:half, GROUP:])
            rest = tall - local
            height = half // parts
            for q in range(parts):
                at = pl.ds(p * PIECE + q * GROUP, GROUP)
                for layer in range(layers):
                    new_mom[layer, :, at] = rest[q * height + layer * own:q * height + (layer + 1) * own]

    loads[2].wait()
    for batch in batches:
        for i in range(1, n_dp):
            dp_arrival(i, batch).wait_recv()
        for p in range(*batch):
            at = pl.ds(p * PIECE, PIECE)
            total = coeffs[0, p]
            for r in range(1, n_dp):
                total += coeffs[r, p]
            high, low = halves(total * (1.0 / n_dp) if n_dp & (n_dp - 1) == 0 else total / n_dp)
            height = high.shape[0]
            left = jnp.concatenate([high, low], axis=0)
            right = jnp.concatenate([high, jnp.zeros_like(low)], axis=0)
            out = dot(jnp.concatenate([left, right], axis=1), w_back[...])
            update = out[:height] + out[height:]
            for layer in range(layers):
                new_par[layer, :, at] = par[layer, :, at] - update[layer * own:(layer + 1) * own]

    for q, p in near_list:
        @pl.when(near_pos < q)
        def _():
            forward(near, q, p).wait_send()

    for q, p in far_list:
        @pl.when(far_pos < q)
        def _():
            forward(far, q, p).wait_send()

    for batch in batches:
        for i in range(1, n_dp):
            dp_copy(i, batch).wait_send()


def store(new_par, new_mom, new_par_hbm, new_mom_hbm, sem):
    copies = [
        pltpu.make_async_copy(new_par, new_par_hbm, sem.at[0]),
        pltpu.make_async_copy(new_mom, new_mom_hbm.at[0], sem.at[1]),
    ]
    for copy in copies:
        copy.start()
    for copy in copies:
        copy.wait()


def shards(n_dp, n_fsdp, grad_partials, momentum, params, kept):
    _, _, layers, rows, cols = grad_partials.shape
    own = rows // n_fsdp
    pieces = cols // PIECE
    batches = ((0, pieces // 2), (pieces // 2, pieces - 1), (pieces - 1, pieces))
    held = (layers, own, cols)
    chunk = (n_fsdp, layers * own, cols)
    anywhere = pl.BlockSpec(memory_space=pl.ANY)
    vmem = pl.BlockSpec(memory_space=pltpu.VMEM)
    inputs = [pltpu.with_memory_space_constraint(x, pltpu.HBM) for x in (grad_partials, momentum, params, kept)]
    sem = pltpu.SemaphoreType.DMA
    results = pl.pallas_call(
        functools.partial(kernel, n_dp, n_fsdp, batches),
        out_shape=(pltpu.VMEM(held, F32), pltpu.VMEM(held, F32)),
        in_specs=[anywhere, anywhere, anywhere, anywhere],
        out_specs=(vmem, vmem),
        scratch_shapes=[
            pltpu.SMEM((KEEP,), jnp.int32),
            pltpu.VMEM((layers, rows, cols), BF16),
            pltpu.VMEM(held, F32),
            pltpu.VMEM(held, F32),
            pltpu.VMEM(chunk, F32),
            pltpu.VMEM((2,) + chunk, F32),
            pltpu.VMEM((n_dp, pieces, layers * own, 128), F32),
            pltpu.VMEM((GROUP, 256), BF16),
            pltpu.VMEM((GROUP, 2 * GROUP), BF16),
            pltpu.VMEM((256, PIECE), BF16),
            sem((4,)),
            sem((2, n_fsdp, pieces)),
            sem((2, n_fsdp, pieces)),
            sem((n_dp, len(batches))),
            sem((n_dp, len(batches))),
        ],
        compiler_params=pltpu.CompilerParams(
            collective_id=0, has_side_effects=True, vmem_limit_bytes=48 * 1024 * 1024
        ),
    )(*inputs)
    results = [pltpu.with_memory_space_constraint(x, pltpu.VMEM) for x in results]
    return pl.pallas_call(
        store,
        out_shape=(
            jax.ShapeDtypeStruct(params.shape, F32),
            jax.ShapeDtypeStruct(momentum.shape, F32),
        ),
        in_specs=[vmem, vmem],
        out_specs=(anywhere, anywhere),
        scratch_shapes=[sem((2,))],
        compiler_params=pltpu.CompilerParams(vmem_limit_bytes=60 * 1024 * 1024),
    )(*results)


def solution(mesh):
    placed = (
        P("dp", "fsdp", None, None, None),
        P("dp", None, "fsdp", None),
        P(None, "fsdp", None),
        P(),
    )
    return jax.shard_map(
        functools.partial(shards, mesh.shape["dp"], mesh.shape["fsdp"]),
        mesh=mesh,
        in_specs=placed,
        out_specs=(P(None, "fsdp", None), P("dp", None, "fsdp", None)),
        check_vma=False,
    )
```

```python
import functools
import math

import jax
import jax.numpy as jnp
from jax import lax
from jax.experimental import pallas as pl
from jax.experimental.pallas import tpu as pltpu
from jax.sharding import PartitionSpec as P

SPAN = 64
KEEP = 8
PIECE = 1024
GROUP = 256
BURST = 5
WINDOW = 3
SUM_DP, SUM_FSDP = 4, 8
LAG = 2
F32 = jnp.float32
BF16 = jnp.bfloat16


def cosine_rows(k, n):
    turn = ((2 * n + 1) * k) & (4 * SPAN - 1)
    turn = jnp.minimum(turn, 4 * SPAN - turn)
    scale = jnp.where(k == 0, math.sqrt(1.0 / SPAN), math.sqrt(2.0 / SPAN)).astype(F32)
    return scale * jnp.cos(turn.astype(F32) * (math.pi / (2 * SPAN)))


def halves(x):
    high = x.astype(BF16)
    return high, (x - high.astype(F32)).astype(BF16)


def dot(a, b):
    return jnp.dot(a, b, preferred_element_type=F32)


def kernel(
    n_dp, n_fsdp,
    grad_hbm, mom_hbm, par_hbm, kept_hbm, new_par, new_mom,
    kept_ref, grad, mom, par, mine, inbox, own_coef, dp_parts, dp_sum, fsdp_parts, total, w_coef, w_proj, w_back,
    load_sem, send_sem, recv_sem, first_send, first_recv, second_send, second_recv, third_send, third_recv,
):
    layers, rows, cols = grad.shape
    own = rows // n_fsdp
    pieces = cols // PIECE
    parts = PIECE // GROUP
    lanes = 128
    dp, me = lax.axis_index("dp"), lax.axis_index("fsdp")
    mesh_id = pl.DeviceIdType.MESH

    loads = [
        pltpu.make_async_copy(kept_hbm, kept_ref, load_sem.at[0]),
        pltpu.make_async_copy(grad_hbm.at[0, 0], grad, load_sem.at[1]),
        pltpu.make_async_copy(mom_hbm.at[0], mom, load_sem.at[2]),
        pltpu.make_async_copy(par_hbm, par, load_sem.at[3]),
    ]
    for load in loads:
        load.start()

    barrier = pltpu.get_barrier_semaphore()
    for i in range(1, n_fsdp):
        pl.semaphore_signal(barrier, inc=1, device_id={"fsdp": lax.rem(me + i, n_fsdp)}, device_id_type=mesh_id)
    for i in range(1, n_dp):
        pl.semaphore_signal(barrier, inc=1, device_id={"dp": lax.rem(dp + i, n_dp)}, device_id_type=mesh_id)

    near = me // (n_fsdp // 2)
    far = 1 - near
    near_pos = near * (n_fsdp - 1 - me) + far * me
    far_pos = n_fsdp - 1 - near_pos

    loads[0].wait()

    def by_index(shape, dim):
        j = lax.broadcasted_iota(jnp.int32, shape, dim) % KEEP
        k = jnp.zeros(shape, jnp.int32)
        for i in range(KEEP):
            k = jnp.where(j == i, kept_ref[i], k)
        return k

    row = cosine_rows(by_index((KEEP, lanes), 0), lax.broadcasted_iota(jnp.int32, (KEEP, lanes), 1) % SPAN)
    column = cosine_rows(by_index((SPAN, lanes), 1), lax.broadcasted_iota(jnp.int32, (SPAN, lanes), 0))
    lane_block = lax.broadcasted_iota(jnp.int32, (SPAN, lanes), 1) // KEEP
    coef = jnp.concatenate([jnp.where(lane_block == b, column, 0.0) for b in range(GROUP // SPAN)], axis=0)
    wide = jnp.concatenate([row] * (PIECE // lanes), axis=1)
    wide_block = lax.broadcasted_iota(jnp.int32, (KEEP, PIECE), 1) // SPAN
    back = jnp.concatenate([jnp.where(wide_block == b, wide, 0.0) for b in range(PIECE // SPAN)], axis=0)
    high, low = halves(coef)
    w_coef[:, :lanes] = high
    w_coef[:, lanes:] = low
    high, low = halves(back)
    w_back[:lanes] = high
    w_back[lanes:] = low

    loads[1].wait()
    for layer in range(layers):
        for p in range(pieces):
            at = pl.ds(p * PIECE, PIECE)
            x = grad[layer, :, at].astype(F32)
            for d in range(n_fsdp):
                mine[d, layer * own:(layer + 1) * own, at] = x[d * own:(d + 1) * own]

    pl.semaphore_wait(barrier, n_dp - 1 + n_fsdp - 1)

    def forward(flow, q, p):
        at = pl.ds(p * PIECE, PIECE)
        d = flow * (n_fsdp - 1 - q) + (1 - flow) * q
        return pltpu.make_async_remote_copy(
            src_ref=mine.at[d, :, at], dst_ref=inbox.at[flow, d, :, at],
            send_sem=send_sem.at[flow, q, p], recv_sem=recv_sem.at[flow, q, p],
            device_id={"fsdp": me + 1 - 2 * flow}, device_id_type=mesh_id,
        )

    def add(flow, q, p):
        at = pl.ds(p * PIECE, PIECE)
        d = flow * (n_fsdp - 1 - q) + (1 - flow) * q
        forward(flow, q, p).wait_recv()
        mine[d, :, at] += inbox[flow, d, :, at]

    near_list = [(q, p) for q in range(n_fsdp - 1, 0, -1) for p in range(pieces)]
    far_list = [(q, p) for q in range(n_fsdp - 1, n_fsdp // 2, -1) for p in range(pieces)]
    burst = min(BURST, len(near_list))

    @pl.when(near_pos == 0)
    def _():
        for q, p in near_list[:burst]:
            forward(near, q, p).start()

    def first_copy(p):
        return pltpu.make_async_remote_copy(
            src_ref=own_coef.at[p], dst_ref=dp_parts.at[dp],
            send_sem=first_send.at[p], recv_sem=first_recv.at[dp],
            device_id={"dp": p}, device_id_type=mesh_id,
        )

    def first_arrival(source):
        return pltpu.make_async_remote_copy(
            src_ref=own_coef.at[0], dst_ref=dp_parts.at[source],
            send_sem=first_send.at[0], recv_sem=first_recv.at[source],
            device_id={"dp": source}, device_id_type=mesh_id,
        )

    def second_copy(i):
        target = lax.rem(me + i, n_fsdp)
        return pltpu.make_async_remote_copy(
            src_ref=dp_sum.at[target], dst_ref=fsdp_parts.at[me],
            send_sem=second_send.at[i], recv_sem=second_recv.at[me],
            device_id={"fsdp": target}, device_id_type=mesh_id,
        )

    def second_arrival(source):
        return pltpu.make_async_remote_copy(
            src_ref=dp_sum.at[0], dst_ref=fsdp_parts.at[source],
            send_sem=second_send.at[0], recv_sem=second_recv.at[source],
            device_id={"fsdp": source}, device_id_type=mesh_id,
        )

    def third_copy(i):
        return pltpu.make_async_remote_copy(
            src_ref=total.at[dp], dst_ref=total.at[dp],
            send_sem=third_send.at[i], recv_sem=third_recv.at[dp],
            device_id={"dp": lax.rem(dp + i, n_dp)}, device_id_type=mesh_id,
        )

    def third_arrival(p):
        return pltpu.make_async_remote_copy(
            src_ref=total.at[p], dst_ref=total.at[p],
            send_sem=third_send.at[0], recv_sem=third_recv.at[p],
            device_id={"dp": p}, device_id_type=mesh_id,
        )

    def pack(out, height):
        packed = out[:height]
        for q in range(1, parts):
            packed += pltpu.roll(out[q * height:(q + 1) * height], q * (lanes // parts), 1)
        return packed

    def state(p):
        at = pl.ds(p * PIECE, PIECE)
        return 0.9 * jnp.concatenate([mom[layer, :, at] for layer in range(layers)], axis=0)

    def stacked(x):
        return jnp.concatenate([x[:, q * GROUP:(q + 1) * GROUP] for q in range(parts)], axis=0)

    loads[2].wait()
    for p in range(pieces):
        tall = [stacked(grad[layer, :, pl.ds(p * PIECE, PIECE)]) for layer in range(layers)]
        tall += list(halves(stacked(state(p))))
        out = dot(jnp.concatenate(tall, axis=0), w_coef[...])
        out = out[:, :lanes] + out[:, lanes:]
        step = parts * rows
        for layer in range(layers):
            packed = pack(out[layer * step:(layer + 1) * step], rows)
            for d in range(n_fsdp):
                own_coef[p, d, layer * own:(layer + 1) * own] = packed[d * own:(d + 1) * own]
        out = out[layers * step:]
        height = layers * own
        own_coef[p, me] += pack(out[:parts * height] + out[parts * height:], height)

        @pl.when(dp != p)
        def _():
            first_copy(p).start()

    proj = jnp.dot(coef, back[:, :GROUP], precision=lax.Precision.HIGHEST, preferred_element_type=F32)
    high, low = halves(proj)
    w_proj[:, :GROUP] = high
    w_proj[:, GROUP:] = low

    def sum_dp():
        @pl.when(dp < pieces)
        def _():
            dp_parts[dp] = own_coef[dp]
            for i in range(1, n_dp):
                first_arrival(lax.rem(dp + i, n_dp)).wait_recv()
            for d in range(n_fsdp):
                value = dp_parts[0, d]
                for r in range(1, n_dp):
                    value += dp_parts[r, d]
                dp_sum[d] = value
            for i in range(1, n_fsdp):
                second_copy(i).start()

    def sum_fsdp():
        @pl.when(dp < pieces)
        def _():
            fsdp_parts[me] = dp_sum[me]
            for i in range(1, n_fsdp):
                second_arrival(lax.rem(me + i, n_fsdp)).wait_recv()
            value = fsdp_parts[0]
            for f in range(1, n_fsdp):
                value += fsdp_parts[f]
            total[dp] = value
            for i in range(1, n_dp):
                third_copy(i).start()

    def update_params():
        for p in range(pieces):
            @pl.when(dp != p)
            def _():
                third_arrival(p).wait_recv()
        shared = jnp.concatenate([total[p] for p in range(pieces)], axis=0) / n_dp
        high, low = halves(shared)
        left = jnp.concatenate([high, low], axis=0)
        right = jnp.concatenate([high, jnp.zeros_like(low)], axis=0)
        out = dot(jnp.concatenate([left, right], axis=1), w_back[...])
        half = shared.shape[0]
        update = out[:half] + out[half:]
        height = layers * own
        loads[3].wait()
        for p in range(pieces):
            at = pl.ds(p * PIECE, PIECE)
            for layer in range(layers):
                top = p * height + layer * own
                new_par[layer, :, at] = par[layer, :, at] - update[top:top + own]

    def near_step(i):
        q, p = near_list[i]

        if i >= burst:
            @pl.when(near_pos == 0)
            def _():
                for j in range(max(0, burst - WINDOW) if i > burst else 0, i - WINDOW + 1):
                    if i == burst or j == i - WINDOW:
                        forward(near, *near_list[j]).wait_send()
                forward(near, q, p).start()

        if q > 1:
            @pl.when((near_pos > 0) & (near_pos < q))
            def _():
                add(near, q, p)
                forward(near, q, p).start()

    def far_step(q, p):
        @pl.when(far_pos < q)
        def _():
            add(far, q, p)
            forward(far, q, p).start()

    for i in range(len(near_list)):
        near_step(i)
        if 0 <= i - LAG < len(far_list):
            far_step(*far_list[i - LAG])
        if i == min(SUM_DP, len(near_list) - 1):
            sum_dp()
        if i == min(SUM_FSDP, len(near_list) - 1):
            sum_fsdp()

    def finish_sends():
        for q, p in near_list:
            @pl.when((near_pos > 0) & (near_pos < q))
            def _():
                forward(near, q, p).wait_send()
        for q, p in far_list:
            @pl.when(far_pos < q)
            def _():
                forward(far, q, p).wait_send()
        for p in range(pieces):
            @pl.when(dp != p)
            def _():
                first_copy(p).wait_send()

        @pl.when(dp < pieces)
        def _():
            for i in range(1, n_fsdp):
                second_copy(i).wait_send()
            for i in range(1, n_dp):
                third_copy(i).wait_send()

    for p in range(pieces):
        if p == pieces - 2:
            update_params()
        if p == pieces - 1:
            finish_sends()
        add(far, far_pos, p)

        @pl.when(near_pos > 0)
        def _():
            add(near, near_pos, p)

        tall = stacked(state(p) + mine[me, :, pl.ds(p * PIECE, PIECE)])
        half = tall.shape[0]
        out = dot(jnp.concatenate(halves(tall), axis=0), w_proj[...])
        rest = tall - (out[:half, :GROUP] + (out[half:, :GROUP] + out[:half, GROUP:]))
        height = half // parts
        for q in range(parts):
            at = pl.ds(p * PIECE + q * GROUP, GROUP)
            for layer in range(layers):
                new_mom[layer, :, at] = rest[q * height + layer * own:q * height + (layer + 1) * own]

    @pl.when(near_pos == 0)
    def _():
        left = len(near_list) - WINDOW if len(near_list) > burst else 0
        for q, p in near_list[left:]:
            forward(near, q, p).wait_send()


def store(new_par, new_mom, new_par_hbm, new_mom_hbm, sem):
    copies = [
        pltpu.make_async_copy(new_par, new_par_hbm, sem.at[0]),
        pltpu.make_async_copy(new_mom, new_mom_hbm.at[0], sem.at[1]),
    ]
    for copy in copies:
        copy.start()
    for copy in copies:
        copy.wait()


def shards(n_dp, n_fsdp, grad_partials, momentum, params, kept):
    _, _, layers, rows, cols = grad_partials.shape
    own = rows // n_fsdp
    pieces = cols // PIECE
    held = (layers, own, cols)
    tile = (layers * own, 128)
    chunk = (n_fsdp, layers * own, cols)
    anywhere = pl.BlockSpec(memory_space=pl.ANY)
    vmem = pl.BlockSpec(memory_space=pltpu.VMEM)
    inputs = [pltpu.with_memory_space_constraint(x, pltpu.HBM) for x in (grad_partials, momentum, params, kept)]
    sem = pltpu.SemaphoreType.DMA
    results = pl.pallas_call(
        functools.partial(kernel, n_dp, n_fsdp),
        out_shape=(pltpu.VMEM(held, F32), pltpu.VMEM(held, F32)),
        in_specs=[anywhere, anywhere, anywhere, anywhere],
        out_specs=(vmem, vmem),
        scratch_shapes=[
            pltpu.SMEM((KEEP,), jnp.int32),
            pltpu.VMEM((layers, rows, cols), BF16),
            pltpu.VMEM(held, F32),
            pltpu.VMEM(held, F32),
            pltpu.VMEM(chunk, F32),
            pltpu.VMEM((2,) + chunk, F32),
            pltpu.VMEM((pieces, n_fsdp) + tile, F32),
            pltpu.VMEM((n_dp, n_fsdp) + tile, F32),
            pltpu.VMEM((n_fsdp,) + tile, F32),
            pltpu.VMEM((n_fsdp,) + tile, F32),
            pltpu.VMEM((pieces,) + tile, F32),
            pltpu.VMEM((GROUP, 256), BF16),
            pltpu.VMEM((GROUP, 2 * GROUP), BF16),
            pltpu.VMEM((256, PIECE), BF16),
            sem((4,)),
            sem((2, n_fsdp, pieces)),
            sem((2, n_fsdp, pieces)),
            sem((pieces,)),
            sem((n_dp,)),
            sem((n_fsdp,)),
            sem((n_fsdp,)),
            sem((n_dp,)),
            sem((pieces,)),
        ],
        compiler_params=pltpu.CompilerParams(
            collective_id=0, has_side_effects=True, vmem_limit_bytes=48 * 1024 * 1024
        ),
    )(*inputs)
    results = [pltpu.with_memory_space_constraint(x, pltpu.VMEM) for x in results]
    return pl.pallas_call(
        store,
        out_shape=(
            jax.ShapeDtypeStruct(params.shape, F32),
            jax.ShapeDtypeStruct(momentum.shape, F32),
        ),
        in_specs=[vmem, vmem],
        out_specs=(anywhere, anywhere),
        scratch_shapes=[sem((2,))],
        compiler_params=pltpu.CompilerParams(vmem_limit_bytes=60 * 1024 * 1024),
    )(*results)


def solution(mesh):
    placed = (
        P("dp", "fsdp", None, None, None),
        P("dp", None, "fsdp", None),
        P(None, "fsdp", None),
        P(),
    )
    return jax.shard_map(
        functools.partial(shards, mesh.shape["dp"], mesh.shape["fsdp"]),
        mesh=mesh,
        in_specs=placed,
        out_specs=(P(None, "fsdp", None), P("dp", None, "fsdp", None)),
        check_vma=False,
    )
```

```python
import functools
import math

import jax
import jax.numpy as jnp
from jax import lax
from jax.experimental import pallas as pl
from jax.experimental.pallas import tpu as pltpu
from jax.sharding import PartitionSpec as P

SPAN = 64
KEEP = 8
PIECE = 1024
GROUP = 256
BURST = 7
SUM_DP, SUM_FSDP = 2, 8
LAG = 2
F32 = jnp.float32
BF16 = jnp.bfloat16


def cosine_rows(k, n):
    turn = ((2 * n + 1) * k) & (4 * SPAN - 1)
    turn = jnp.minimum(turn, 4 * SPAN - turn)
    scale = jnp.where(k == 0, math.sqrt(1.0 / SPAN), math.sqrt(2.0 / SPAN)).astype(F32)
    return scale * jnp.cos(turn.astype(F32) * (math.pi / (2 * SPAN)))


def halves(x):
    high = x.astype(BF16)
    return high, (x - high.astype(F32)).astype(BF16)


def dot(a, b):
    return jnp.dot(a, b, preferred_element_type=F32)


def kernel(
    n_dp, n_fsdp,
    grad_hbm, mom_hbm, par_hbm, kept_hbm, new_par, new_mom,
    kept_ref, grad, mom, par, mine, inbox, own_coef, dp_parts, dp_sum, fsdp_parts, total, w_coef, w_proj, w_back,
    load_sem, send_sem, recv_sem, first_send, first_recv, second_send, second_recv, third_send, third_recv,
):
    layers, rows, cols = grad.shape
    own = rows // n_fsdp
    pieces = cols // PIECE
    parts = PIECE // GROUP
    lanes = 128
    dp, me = lax.axis_index("dp"), lax.axis_index("fsdp")
    mesh_id = pl.DeviceIdType.MESH

    loads = [
        pltpu.make_async_copy(kept_hbm, kept_ref, load_sem.at[0]),
        pltpu.make_async_copy(grad_hbm.at[0, 0], grad, load_sem.at[1]),
        pltpu.make_async_copy(mom_hbm.at[0], mom, load_sem.at[2]),
        pltpu.make_async_copy(par_hbm, par, load_sem.at[3]),
    ]
    for load in loads:
        load.start()

    barrier = pltpu.get_barrier_semaphore()
    for i in range(1, n_fsdp):
        pl.semaphore_signal(barrier, inc=1, device_id={"fsdp": lax.rem(me + i, n_fsdp)}, device_id_type=mesh_id)
    for i in range(1, n_dp):
        pl.semaphore_signal(barrier, inc=1, device_id={"dp": lax.rem(dp + i, n_dp)}, device_id_type=mesh_id)

    near = me // (n_fsdp // 2)
    far = 1 - near
    near_pos = near * (n_fsdp - 1 - me) + far * me
    far_pos = n_fsdp - 1 - near_pos

    loads[1].wait()
    for layer in range(layers):
        for p in range(pieces):
            at = pl.ds(p * PIECE, PIECE)
            x = grad[layer, :, at].astype(F32)
            for d in range(n_fsdp):
                mine[d, layer * own:(layer + 1) * own, at] = x[d * own:(d + 1) * own]

    pl.semaphore_wait(barrier, n_dp - 1 + n_fsdp - 1)

    def forward(flow, q, p):
        at = pl.ds(p * PIECE, PIECE)
        d = flow * (n_fsdp - 1 - q) + (1 - flow) * q
        return pltpu.make_async_remote_copy(
            src_ref=mine.at[d, :, at], dst_ref=inbox.at[flow, d, :, at],
            send_sem=send_sem.at[flow, q, p], recv_sem=recv_sem.at[flow, q, p],
            device_id={"fsdp": me + 1 - 2 * flow}, device_id_type=mesh_id,
        )

    def add(flow, q, p):
        at = pl.ds(p * PIECE, PIECE)
        d = flow * (n_fsdp - 1 - q) + (1 - flow) * q
        forward(flow, q, p).wait_recv()
        mine[d, :, at] += inbox[flow, d, :, at]

    near_list = [(q, p) for q in range(n_fsdp - 1, 0, -1) for p in range(pieces)]
    far_list = [(q, p) for q in range(n_fsdp - 1, n_fsdp // 2, -1) for p in range(pieces)]
    burst = min(BURST, len(near_list))

    @pl.when(near_pos == 0)
    def _():
        for q, p in near_list[:burst]:
            forward(near, q, p).start()

    loads[0].wait()

    def by_index(shape, dim):
        j = lax.broadcasted_iota(jnp.int32, shape, dim) % KEEP
        k = jnp.zeros(shape, jnp.int32)
        for i in range(KEEP):
            k = jnp.where(j == i, kept_ref[i], k)
        return k

    row = cosine_rows(by_index((KEEP, lanes), 0), lax.broadcasted_iota(jnp.int32, (KEEP, lanes), 1) % SPAN)
    column = cosine_rows(by_index((SPAN, lanes), 1), lax.broadcasted_iota(jnp.int32, (SPAN, lanes), 0))
    lane_block = lax.broadcasted_iota(jnp.int32, (SPAN, lanes), 1) // KEEP
    coef = jnp.concatenate([jnp.where(lane_block == b, column, 0.0) for b in range(GROUP // SPAN)], axis=0)
    wide = jnp.concatenate([row] * (PIECE // lanes), axis=1)
    wide_block = lax.broadcasted_iota(jnp.int32, (KEEP, PIECE), 1) // SPAN
    back = jnp.concatenate([jnp.where(wide_block == b, wide, 0.0) for b in range(PIECE // SPAN)], axis=0)
    high, low = halves(coef)
    w_coef[:, :lanes] = high
    w_coef[:, lanes:] = low
    high, low = halves(back)
    w_back[:lanes] = high
    w_back[lanes:] = low

    def first_copy(p):
        return pltpu.make_async_remote_copy(
            src_ref=own_coef.at[p], dst_ref=dp_parts.at[dp],
            send_sem=first_send.at[p], recv_sem=first_recv.at[dp],
            device_id={"dp": p}, device_id_type=mesh_id,
        )

    def first_arrival(source):
        return pltpu.make_async_remote_copy(
            src_ref=own_coef.at[0], dst_ref=dp_parts.at[source],
            send_sem=first_send.at[0], recv_sem=first_recv.at[source],
            device_id={"dp": source}, device_id_type=mesh_id,
        )

    def second_copy(i):
        target = lax.rem(me + i, n_fsdp)
        return pltpu.make_async_remote_copy(
            src_ref=dp_sum.at[target], dst_ref=fsdp_parts.at[me],
            send_sem=second_send.at[i], recv_sem=second_recv.at[me],
            device_id={"fsdp": target}, device_id_type=mesh_id,
        )

    def second_arrival(source):
        return pltpu.make_async_remote_copy(
            src_ref=dp_sum.at[0], dst_ref=fsdp_parts.at[source],
            send_sem=second_send.at[0], recv_sem=second_recv.at[source],
            device_id={"fsdp": source}, device_id_type=mesh_id,
        )

    def third_copy(i):
        return pltpu.make_async_remote_copy(
            src_ref=total.at[dp], dst_ref=total.at[dp],
            send_sem=third_send.at[i], recv_sem=third_recv.at[dp],
            device_id={"dp": lax.rem(dp + i, n_dp)}, device_id_type=mesh_id,
        )

    def third_arrival(p):
        return pltpu.make_async_remote_copy(
            src_ref=total.at[p], dst_ref=total.at[p],
            send_sem=third_send.at[0], recv_sem=third_recv.at[p],
            device_id={"dp": p}, device_id_type=mesh_id,
        )

    def pack(out, height):
        packed = out[:height]
        for q in range(1, parts):
            packed += pltpu.roll(out[q * height:(q + 1) * height], q * (lanes // parts), 1)
        return packed

    def state(p):
        at = pl.ds(p * PIECE, PIECE)
        return 0.9 * jnp.concatenate([mom[layer, :, at] for layer in range(layers)], axis=0)

    def stacked(x):
        return jnp.concatenate([x[:, q * GROUP:(q + 1) * GROUP] for q in range(parts)], axis=0)

    loads[2].wait()
    for p in range(pieces):
        tall = [stacked(grad[layer, :, pl.ds(p * PIECE, PIECE)]) for layer in range(layers)]
        tall += list(halves(stacked(state(p))))
        out = dot(jnp.concatenate(tall, axis=0), w_coef[...])
        out = out[:, :lanes] + out[:, lanes:]
        step = parts * rows
        for layer in range(layers):
            packed = pack(out[layer * step:(layer + 1) * step], rows)
            for d in range(n_fsdp):
                own_coef[p, d, layer * own:(layer + 1) * own] = packed[d * own:(d + 1) * own]
        out = out[layers * step:]
        height = layers * own
        own_coef[p, me] += pack(out[:parts * height] + out[parts * height:], height)

        @pl.when(dp != p)
        def _():
            first_copy(p).start()

    proj = jnp.dot(coef, back[:, :GROUP], precision=lax.Precision.HIGHEST, preferred_element_type=F32)
    high, low = halves(proj)
    w_proj[:, :GROUP] = high
    w_proj[:, GROUP:] = low

    def sum_dp():
        @pl.when(dp < pieces)
        def _():
            dp_parts[dp] = own_coef[dp]
            for i in range(1, n_dp):
                first_arrival(lax.rem(dp + i, n_dp)).wait_recv()
            for d in range(n_fsdp):
                value = dp_parts[0, d]
                for r in range(1, n_dp):
                    value += dp_parts[r, d]
                dp_sum[d] = value
            for i in range(1, n_fsdp):
                second_copy(i).start()

    def sum_fsdp():
        @pl.when(dp < pieces)
        def _():
            fsdp_parts[me] = dp_sum[me]
            for i in range(1, n_fsdp):
                second_arrival(lax.rem(me + i, n_fsdp)).wait_recv()
            value = fsdp_parts[0]
            for f in range(1, n_fsdp):
                value += fsdp_parts[f]
            total[dp] = value
            for i in range(1, n_dp):
                third_copy(i).start()

    def update_params():
        for p in range(pieces):
            @pl.when(dp != p)
            def _():
                third_arrival(p).wait_recv()
        shared = jnp.concatenate([total[p] for p in range(pieces)], axis=0) / n_dp
        high, low = halves(shared)
        left = jnp.concatenate([high, low], axis=0)
        right = jnp.concatenate([high, jnp.zeros_like(low)], axis=0)
        out = dot(jnp.concatenate([left, right], axis=1), w_back[...])
        half = shared.shape[0]
        update = out[:half] + out[half:]
        height = layers * own
        loads[3].wait()
        for p in range(pieces):
            at = pl.ds(p * PIECE, PIECE)
            for layer in range(layers):
                top = p * height + layer * own
                new_par[layer, :, at] = par[layer, :, at] - update[top:top + own]

    def near_step(i):
        q, p = near_list[i]

        if q > 1:
            @pl.when((near_pos > 0) & (near_pos < q))
            def _():
                add(near, q, p)
                forward(near, q, p).start()

    def far_step(q, p):
        @pl.when(far_pos < q)
        def _():
            add(far, q, p)
            forward(far, q, p).start()

    @pl.when(near_pos == 0)
    def _():
        sum_dp()
        for q, p in near_list[burst:]:
            forward(near, q, p).start()
        sum_fsdp()

    for i in range(len(near_list)):
        near_step(i)
        if 0 <= i - LAG < len(far_list):
            far_step(*far_list[i - LAG])
        if i == min(SUM_DP, len(near_list) - 1):
            pl.when(near_pos > 0)(sum_dp)
        if i == min(SUM_FSDP, len(near_list) - 1):
            pl.when(near_pos > 0)(sum_fsdp)

    def finish_sends():
        for q, p in near_list:
            @pl.when((near_pos > 0) & (near_pos < q))
            def _():
                forward(near, q, p).wait_send()
        for q, p in far_list:
            @pl.when(far_pos < q)
            def _():
                forward(far, q, p).wait_send()
        for p in range(pieces):
            @pl.when(dp != p)
            def _():
                first_copy(p).wait_send()

        @pl.when(dp < pieces)
        def _():
            for i in range(1, n_fsdp):
                second_copy(i).wait_send()
            for i in range(1, n_dp):
                third_copy(i).wait_send()

    for p in range(pieces):
        if p == pieces - 2:
            update_params()
        if p == pieces - 1:
            finish_sends()
        add(far, far_pos, p)

        @pl.when(near_pos > 0)
        def _():
            add(near, near_pos, p)

        tall = stacked(state(p) + mine[me, :, pl.ds(p * PIECE, PIECE)])
        half = tall.shape[0]
        out = dot(jnp.concatenate(halves(tall), axis=0), w_proj[...])
        rest = tall - (out[:half, :GROUP] + (out[half:, :GROUP] + out[:half, GROUP:]))
        height = half // parts
        for q in range(parts):
            at = pl.ds(p * PIECE + q * GROUP, GROUP)
            for layer in range(layers):
                new_mom[layer, :, at] = rest[q * height + layer * own:q * height + (layer + 1) * own]

    @pl.when(near_pos == 0)
    def _():
        for q, p in near_list:
            forward(near, q, p).wait_send()


def store(new_par, new_mom, new_par_hbm, new_mom_hbm, sem):
    copies = [
        pltpu.make_async_copy(new_par, new_par_hbm, sem.at[0]),
        pltpu.make_async_copy(new_mom, new_mom_hbm.at[0], sem.at[1]),
    ]
    for copy in copies:
        copy.start()
    for copy in copies:
        copy.wait()


def shards(n_dp, n_fsdp, grad_partials, momentum, params, kept):
    _, _, layers, rows, cols = grad_partials.shape
    own = rows // n_fsdp
    pieces = cols // PIECE
    held = (layers, own, cols)
    tile = (layers * own, 128)
    chunk = (n_fsdp, layers * own, cols)
    anywhere = pl.BlockSpec(memory_space=pl.ANY)
    vmem = pl.BlockSpec(memory_space=pltpu.VMEM)
    inputs = [pltpu.with_memory_space_constraint(x, pltpu.HBM) for x in (grad_partials, momentum, params, kept)]
    sem = pltpu.SemaphoreType.DMA
    results = pl.pallas_call(
        functools.partial(kernel, n_dp, n_fsdp),
        out_shape=(pltpu.VMEM(held, F32), pltpu.VMEM(held, F32)),
        in_specs=[anywhere, anywhere, anywhere, anywhere],
        out_specs=(vmem, vmem),
        scratch_shapes=[
            pltpu.SMEM((KEEP,), jnp.int32),
            pltpu.VMEM((layers, rows, cols), BF16),
            pltpu.VMEM(held, F32),
            pltpu.VMEM(held, F32),
            pltpu.VMEM(chunk, F32),
            pltpu.VMEM((2,) + chunk, F32),
            pltpu.VMEM((pieces, n_fsdp) + tile, F32),
            pltpu.VMEM((n_dp, n_fsdp) + tile, F32),
            pltpu.VMEM((n_fsdp,) + tile, F32),
            pltpu.VMEM((n_fsdp,) + tile, F32),
            pltpu.VMEM((pieces,) + tile, F32),
            pltpu.VMEM((GROUP, 256), BF16),
            pltpu.VMEM((GROUP, 2 * GROUP), BF16),
            pltpu.VMEM((256, PIECE), BF16),
            sem((4,)),
            sem((2, n_fsdp, pieces)),
            sem((2, n_fsdp, pieces)),
            sem((pieces,)),
            sem((n_dp,)),
            sem((n_fsdp,)),
            sem((n_fsdp,)),
            sem((n_dp,)),
            sem((pieces,)),
        ],
        compiler_params=pltpu.CompilerParams(
            collective_id=0, has_side_effects=True, vmem_limit_bytes=48 * 1024 * 1024
        ),
    )(*inputs)
    results = [pltpu.with_memory_space_constraint(x, pltpu.VMEM) for x in results]
    return pl.pallas_call(
        store,
        out_shape=(
            jax.ShapeDtypeStruct(params.shape, F32),
            jax.ShapeDtypeStruct(momentum.shape, F32),
        ),
        in_specs=[vmem, vmem],
        out_specs=(anywhere, anywhere),
        scratch_shapes=[sem((2,))],
        compiler_params=pltpu.CompilerParams(vmem_limit_bytes=60 * 1024 * 1024),
    )(*results)


def solution(mesh):
    placed = (
        P("dp", "fsdp", None, None, None),
        P("dp", None, "fsdp", None),
        P(None, "fsdp", None),
        P(),
    )
    return jax.shard_map(
        functools.partial(shards, mesh.shape["dp"], mesh.shape["fsdp"]),
        mesh=mesh,
        in_specs=placed,
        out_specs=(P(None, "fsdp", None), P("dp", None, "fsdp", None)),
        check_vma=False,
    )
```

```python
import functools
import math

import jax
import jax.numpy as jnp
from jax import lax
from jax.experimental import pallas as pl
from jax.experimental.pallas import tpu as pltpu
from jax.sharding import PartitionSpec as P

SPAN = 64
KEEP = 8
PIECE = 1024
GROUP = 256
BURST = 6
SUM_DP, SUM_FSDP = 2, 7
LAG = 2
F32 = jnp.float32
BF16 = jnp.bfloat16


def cosine_rows(k, n):
    turn = ((2 * n + 1) * k) & (4 * SPAN - 1)
    turn = jnp.minimum(turn, 4 * SPAN - turn)
    scale = jnp.where(k == 0, math.sqrt(1.0 / SPAN), math.sqrt(2.0 / SPAN)).astype(F32)
    return scale * jnp.cos(turn.astype(F32) * (math.pi / (2 * SPAN)))


def halves(x):
    high = x.astype(BF16)
    return high, (x - high.astype(F32)).astype(BF16)


def dot(a, b):
    return jnp.dot(a, b, preferred_element_type=F32)


def kernel(
    n_dp, n_fsdp,
    grad_hbm, mom_hbm, par_hbm, kept_hbm, new_par, new_mom,
    kept_ref, grad, mom, par, mine, inbox, own_coef, dp_parts, dp_sum, fsdp_parts, total, w_coef, w_proj, w_back,
    load_sem, send_sem, recv_sem, first_send, first_recv, second_send, second_recv, third_send, third_recv,
):
    layers, rows, cols = grad.shape
    own = rows // n_fsdp
    pieces = cols // PIECE
    parts = PIECE // GROUP
    lanes = 128
    dp, me = lax.axis_index("dp"), lax.axis_index("fsdp")
    mesh_id = pl.DeviceIdType.MESH

    loads = [
        pltpu.make_async_copy(kept_hbm, kept_ref, load_sem.at[0]),
        pltpu.make_async_copy(grad_hbm.at[0, 0], grad, load_sem.at[1]),
        pltpu.make_async_copy(mom_hbm.at[0], mom, load_sem.at[2]),
        pltpu.make_async_copy(par_hbm, par, load_sem.at[3]),
    ]
    for load in loads:
        load.start()

    barrier = pltpu.get_barrier_semaphore()
    for i in range(1, n_fsdp):
        pl.semaphore_signal(barrier, inc=1, device_id={"fsdp": lax.rem(me + i, n_fsdp)}, device_id_type=mesh_id)
    for i in range(1, n_dp):
        pl.semaphore_signal(barrier, inc=1, device_id={"dp": lax.rem(dp + i, n_dp)}, device_id_type=mesh_id)

    near = me // (n_fsdp // 2)
    far = 1 - near
    near_pos = near * (n_fsdp - 1 - me) + far * me
    far_pos = n_fsdp - 1 - near_pos

    loads[1].wait()
    for layer in range(layers):
        for p in range(pieces):
            at = pl.ds(p * PIECE, PIECE)
            x = grad[layer, :, at].astype(F32)
            for d in range(n_fsdp):
                mine[d, layer * own:(layer + 1) * own, at] = x[d * own:(d + 1) * own]

    pl.semaphore_wait(barrier, n_dp - 1 + n_fsdp - 1)

    def forward(flow, q, p):
        at = pl.ds(p * PIECE, PIECE)
        d = flow * (n_fsdp - 1 - q) + (1 - flow) * q
        return pltpu.make_async_remote_copy(
            src_ref=mine.at[d, :, at], dst_ref=inbox.at[flow, d, :, at],
            send_sem=send_sem.at[flow, q, p], recv_sem=recv_sem.at[flow, q, p],
            device_id={"fsdp": me + 1 - 2 * flow}, device_id_type=mesh_id,
        )

    def add(flow, q, p):
        at = pl.ds(p * PIECE, PIECE)
        d = flow * (n_fsdp - 1 - q) + (1 - flow) * q
        forward(flow, q, p).wait_recv()
        mine[d, :, at] += inbox[flow, d, :, at]

    near_list = [(q, p) for q in range(n_fsdp - 1, 0, -1) for p in range(pieces)]
    far_list = [(q, p) for q in range(n_fsdp - 1, n_fsdp // 2, -1) for p in range(pieces)]
    burst = min(BURST, len(near_list))

    @pl.when(near_pos == 0)
    def _():
        for q, p in near_list[:burst]:
            forward(near, q, p).start()

    loads[0].wait()

    def by_index(shape, dim):
        j = lax.broadcasted_iota(jnp.int32, shape, dim) % KEEP
        k = jnp.zeros(shape, jnp.int32)
        for i in range(KEEP):
            k = jnp.where(j == i, kept_ref[i], k)
        return k

    row = cosine_rows(by_index((KEEP, lanes), 0), lax.broadcasted_iota(jnp.int32, (KEEP, lanes), 1) % SPAN)
    column = cosine_rows(by_index((SPAN, lanes), 1), lax.broadcasted_iota(jnp.int32, (SPAN, lanes), 0))
    lane_block = lax.broadcasted_iota(jnp.int32, (SPAN, lanes), 1) // KEEP
    coef = jnp.concatenate([jnp.where(lane_block == b, column, 0.0) for b in range(GROUP // SPAN)], axis=0)
    wide = jnp.concatenate([row] * (PIECE // lanes), axis=1)
    wide_block = lax.broadcasted_iota(jnp.int32, (KEEP, PIECE), 1) // SPAN
    back = jnp.concatenate([jnp.where(wide_block == b, wide, 0.0) for b in range(PIECE // SPAN)], axis=0)
    high, low = halves(coef)
    w_coef[:, :lanes] = high
    w_coef[:, lanes:] = low
    high, low = halves(back)
    w_back[:lanes] = high
    w_back[lanes:] = low

    def first_copy(p):
        return pltpu.make_async_remote_copy(
            src_ref=own_coef.at[p], dst_ref=dp_parts.at[dp],
            send_sem=first_send.at[p], recv_sem=first_recv.at[dp],
            device_id={"dp": p}, device_id_type=mesh_id,
        )

    def first_arrival(source):
        return pltpu.make_async_remote_copy(
            src_ref=own_coef.at[0], dst_ref=dp_parts.at[source],
            send_sem=first_send.at[0], recv_sem=first_recv.at[source],
            device_id={"dp": source}, device_id_type=mesh_id,
        )

    def second_copy(i):
        target = lax.rem(me + i, n_fsdp)
        return pltpu.make_async_remote_copy(
            src_ref=dp_sum.at[target], dst_ref=fsdp_parts.at[me],
            send_sem=second_send.at[i], recv_sem=second_recv.at[me],
            device_id={"fsdp": target}, device_id_type=mesh_id,
        )

    def second_arrival(source):
        return pltpu.make_async_remote_copy(
            src_ref=dp_sum.at[0], dst_ref=fsdp_parts.at[source],
            send_sem=second_send.at[0], recv_sem=second_recv.at[source],
            device_id={"fsdp": source}, device_id_type=mesh_id,
        )

    def third_copy(i):
        return pltpu.make_async_remote_copy(
            src_ref=total.at[dp], dst_ref=total.at[dp],
            send_sem=third_send.at[i], recv_sem=third_recv.at[dp],
            device_id={"dp": lax.rem(dp + i, n_dp)}, device_id_type=mesh_id,
        )

    def third_arrival(p):
        return pltpu.make_async_remote_copy(
            src_ref=total.at[p], dst_ref=total.at[p],
            send_sem=third_send.at[0], recv_sem=third_recv.at[p],
            device_id={"dp": p}, device_id_type=mesh_id,
        )

    def pack(out, height):
        packed = out[:height]
        for q in range(1, parts):
            packed += pltpu.roll(out[q * height:(q + 1) * height], q * (lanes // parts), 1)
        return packed

    def state(p):
        at = pl.ds(p * PIECE, PIECE)
        return 0.9 * jnp.concatenate([mom[layer, :, at] for layer in range(layers)], axis=0)

    def stacked(x):
        return jnp.concatenate([x[:, q * GROUP:(q + 1) * GROUP] for q in range(parts)], axis=0)

    loads[2].wait()
    for p in range(pieces):
        tall = [stacked(grad[layer, :, pl.ds(p * PIECE, PIECE)]) for layer in range(layers)]
        tall += list(halves(stacked(state(p))))
        out = dot(jnp.concatenate(tall, axis=0), w_coef[...])
        out = out[:, :lanes] + out[:, lanes:]
        step = parts * rows
        for layer in range(layers):
            packed = pack(out[layer * step:(layer + 1) * step], rows)
            for d in range(n_fsdp):
                own_coef[p, d, layer * own:(layer + 1) * own] = packed[d * own:(d + 1) * own]
        out = out[layers * step:]
        height = layers * own
        own_coef[p, me] += pack(out[:parts * height] + out[parts * height:], height)

        @pl.when(dp != p)
        def _():
            first_copy(p).start()

    proj = jnp.dot(coef, back[:, :GROUP], precision=lax.Precision.HIGHEST, preferred_element_type=F32)
    high, low = halves(proj)
    w_proj[:, :GROUP] = high
    w_proj[:, GROUP:] = low

    def sum_dp():
        @pl.when(dp < pieces)
        def _():
            dp_parts[dp] = own_coef[dp]
            for i in range(1, n_dp):
                first_arrival(lax.rem(dp + i, n_dp)).wait_recv()
            for d in range(n_fsdp):
                value = dp_parts[0, d]
                for r in range(1, n_dp):
                    value += dp_parts[r, d]
                dp_sum[d] = value
            for i in range(1, n_fsdp):
                second_copy(i).start()

    def sum_fsdp():
        @pl.when(dp < pieces)
        def _():
            fsdp_parts[me] = dp_sum[me]
            for i in range(1, n_fsdp):
                second_arrival(lax.rem(me + i, n_fsdp)).wait_recv()
            value = fsdp_parts[0]
            for f in range(1, n_fsdp):
                value += fsdp_parts[f]
            total[dp] = value
            for i in range(1, n_dp):
                third_copy(i).start()

    def update_params():
        for p in range(pieces):
            @pl.when(dp != p)
            def _():
                third_arrival(p).wait_recv()
        shared = jnp.concatenate([total[p] for p in range(pieces)], axis=0) / n_dp
        high, low = halves(shared)
        left = jnp.concatenate([high, low], axis=0)
        right = jnp.concatenate([high, jnp.zeros_like(low)], axis=0)
        out = dot(jnp.concatenate([left, right], axis=1), w_back[...])
        half = shared.shape[0]
        update = out[:half] + out[half:]
        height = layers * own
        loads[3].wait()
        for p in range(pieces):
            at = pl.ds(p * PIECE, PIECE)
            for layer in range(layers):
                top = p * height + layer * own
                new_par[layer, :, at] = par[layer, :, at] - update[top:top + own]

    def near_step(i):
        q, p = near_list[i]

        if q > 1:
            @pl.when((near_pos > 0) & (near_pos < q))
            def _():
                add(near, q, p)
                forward(near, q, p).start()

    def far_step(q, p):
        @pl.when(far_pos < q)
        def _():
            add(far, q, p)
            forward(far, q, p).start()

    @pl.when(near_pos == 0)
    def _():
        sum_dp()
        for q, p in near_list[burst:]:
            forward(near, q, p).start()
        sum_fsdp()

    for i in range(len(near_list)):
        near_step(i)
        if 0 <= i - LAG < len(far_list):
            far_step(*far_list[i - LAG])
        if i == min(SUM_DP, len(near_list) - 1):
            pl.when(near_pos > 0)(sum_dp)
        if i == min(SUM_FSDP, len(near_list) - 1):
            pl.when(near_pos > 0)(sum_fsdp)

    def finish_sends():
        for q, p in near_list:
            @pl.when((near_pos > 0) & (near_pos < q))
            def _():
                forward(near, q, p).wait_send()
        for q, p in far_list:
            @pl.when(far_pos < q)
            def _():
                forward(far, q, p).wait_send()
        for p in range(pieces):
            @pl.when(dp != p)
            def _():
                first_copy(p).wait_send()

        @pl.when(dp < pieces)
        def _():
            for i in range(1, n_fsdp):
                second_copy(i).wait_send()
            for i in range(1, n_dp):
                third_copy(i).wait_send()

    height = layers * own
    groups = [range(p, min(p + 2, pieces)) for p in range(0, pieces, 2)]
    for g, group in enumerate(groups):
        if g == min(1, len(groups) - 1):
            update_params()
        if g == len(groups) - 1:
            finish_sends()
        tall = []
        for p in group:
            add(far, far_pos, p)

            @pl.when(near_pos > 0)
            def _():
                add(near, near_pos, p)

            tall.append(stacked(state(p) + mine[me, :, pl.ds(p * PIECE, PIECE)]))
        tall = jnp.concatenate(tall, axis=0)
        half = tall.shape[0]
        out = dot(jnp.concatenate(halves(tall), axis=0), w_proj[...])
        rest = tall - (out[:half, :GROUP] + (out[half:, :GROUP] + out[:half, GROUP:]))
        for j in range(len(group) * parts):
            at = pl.ds(group[0] * PIECE + j * GROUP, GROUP)
            for layer in range(layers):
                new_mom[layer, :, at] = rest[j * height + layer * own:j * height + (layer + 1) * own]

    @pl.when(near_pos == 0)
    def _():
        for q, p in near_list:
            forward(near, q, p).wait_send()


def store(new_par, new_mom, new_par_hbm, new_mom_hbm, sem):
    copies = [
        pltpu.make_async_copy(new_par, new_par_hbm, sem.at[0]),
        pltpu.make_async_copy(new_mom, new_mom_hbm.at[0], sem.at[1]),
    ]
    for copy in copies:
        copy.start()
    for copy in copies:
        copy.wait()


def shards(n_dp, n_fsdp, grad_partials, momentum, params, kept):
    _, _, layers, rows, cols = grad_partials.shape
    own = rows // n_fsdp
    pieces = cols // PIECE
    held = (layers, own, cols)
    tile = (layers * own, 128)
    chunk = (n_fsdp, layers * own, cols)
    anywhere = pl.BlockSpec(memory_space=pl.ANY)
    vmem = pl.BlockSpec(memory_space=pltpu.VMEM)
    inputs = [pltpu.with_memory_space_constraint(x, pltpu.HBM) for x in (grad_partials, momentum, params, kept)]
    sem = pltpu.SemaphoreType.DMA
    results = pl.pallas_call(
        functools.partial(kernel, n_dp, n_fsdp),
        out_shape=(pltpu.VMEM(held, F32), pltpu.VMEM(held, F32)),
        in_specs=[anywhere, anywhere, anywhere, anywhere],
        out_specs=(vmem, vmem),
        scratch_shapes=[
            pltpu.SMEM((KEEP,), jnp.int32),
            pltpu.VMEM((layers, rows, cols), BF16),
            pltpu.VMEM(held, F32),
            pltpu.VMEM(held, F32),
            pltpu.VMEM(chunk, F32),
            pltpu.VMEM((2,) + chunk, F32),
            pltpu.VMEM((pieces, n_fsdp) + tile, F32),
            pltpu.VMEM((n_dp, n_fsdp) + tile, F32),
            pltpu.VMEM((n_fsdp,) + tile, F32),
            pltpu.VMEM((n_fsdp,) + tile, F32),
            pltpu.VMEM((pieces,) + tile, F32),
            pltpu.VMEM((GROUP, 256), BF16),
            pltpu.VMEM((GROUP, 2 * GROUP), BF16),
            pltpu.VMEM((256, PIECE), BF16),
            sem((4,)),
            sem((2, n_fsdp, pieces)),
            sem((2, n_fsdp, pieces)),
            sem((pieces,)),
            sem((n_dp,)),
            sem((n_fsdp,)),
            sem((n_fsdp,)),
            sem((n_dp,)),
            sem((pieces,)),
        ],
        compiler_params=pltpu.CompilerParams(
            collective_id=0, has_side_effects=True, vmem_limit_bytes=48 * 1024 * 1024
        ),
    )(*inputs)
    results = [pltpu.with_memory_space_constraint(x, pltpu.VMEM) for x in results]
    return pl.pallas_call(
        store,
        out_shape=(
            jax.ShapeDtypeStruct(params.shape, F32),
            jax.ShapeDtypeStruct(momentum.shape, F32),
        ),
        in_specs=[vmem, vmem],
        out_specs=(anywhere, anywhere),
        scratch_shapes=[sem((2,))],
        compiler_params=pltpu.CompilerParams(vmem_limit_bytes=60 * 1024 * 1024),
    )(*results)


def solution(mesh):
    placed = (
        P("dp", "fsdp", None, None, None),
        P("dp", None, "fsdp", None),
        P(None, "fsdp", None),
        P(),
    )
    return jax.shard_map(
        functools.partial(shards, mesh.shape["dp"], mesh.shape["fsdp"]),
        mesh=mesh,
        in_specs=placed,
        out_specs=(P(None, "fsdp", None), P("dp", None, "fsdp", None)),
        check_vma=False,
    )
```

```python
import functools
import math

import jax
import jax.numpy as jnp
from jax import lax
from jax.experimental import pallas as pl
from jax.experimental.pallas import tpu as pltpu
from jax.sharding import PartitionSpec as P

SPAN = 64
KEEP = 8
PIECE = 1024
GROUP = 256
BURST = 6
SUM_DP, SUM_FSDP = 2, 7
LAG = 2
F32 = jnp.float32
BF16 = jnp.bfloat16


def cosine_rows(k, n):
    turn = ((2 * n + 1) * k) & (4 * SPAN - 1)
    turn = jnp.minimum(turn, 4 * SPAN - turn)
    scale = jnp.where(k == 0, math.sqrt(1.0 / SPAN), math.sqrt(2.0 / SPAN)).astype(F32)
    return scale * jnp.cos(turn.astype(F32) * (math.pi / (2 * SPAN)))


def halves(x):
    high = x.astype(BF16)
    return high, (x - high.astype(F32)).astype(BF16)


def dot(a, b):
    return jnp.dot(a, b, preferred_element_type=F32)


def kernel(
    n_dp, n_fsdp,
    grad_hbm, mom_hbm, par_hbm, kept_hbm, new_par, new_mom,
    kept_ref, grad, mom, par, mine, inbox, own_coef, dp_parts, dp_sum, fsdp_parts, total, w_coef, w_proj, w_back,
    load_sem, send_sem, recv_sem, first_send, first_recv, second_send, second_recv, third_send, third_recv,
):
    layers, rows, cols = grad.shape
    own = rows // n_fsdp
    pieces = cols // PIECE
    parts = PIECE // GROUP
    lanes = 128
    dp, me = lax.axis_index("dp"), lax.axis_index("fsdp")
    mesh_id = pl.DeviceIdType.MESH

    loads = [
        pltpu.make_async_copy(kept_hbm, kept_ref, load_sem.at[0]),
        pltpu.make_async_copy(grad_hbm.at[0, 0], grad, load_sem.at[1]),
        pltpu.make_async_copy(mom_hbm.at[0], mom, load_sem.at[2]),
        pltpu.make_async_copy(par_hbm, par, load_sem.at[3]),
    ]
    for load in loads:
        load.start()

    barrier = pltpu.get_barrier_semaphore()
    for i in range(1, n_fsdp):
        pl.semaphore_signal(barrier, inc=1, device_id={"fsdp": lax.rem(me + i, n_fsdp)}, device_id_type=mesh_id)
    for i in range(1, n_dp):
        pl.semaphore_signal(barrier, inc=1, device_id={"dp": lax.rem(dp + i, n_dp)}, device_id_type=mesh_id)

    near = me // (n_fsdp // 2)
    far = 1 - near
    near_pos = near * (n_fsdp - 1 - me) + far * me
    far_pos = n_fsdp - 1 - near_pos

    def forward(flow, q, p):
        at = pl.ds(p * PIECE, PIECE)
        d = flow * (n_fsdp - 1 - q) + (1 - flow) * q
        return pltpu.make_async_remote_copy(
            src_ref=mine.at[d, :, at], dst_ref=inbox.at[flow, d, :, at],
            send_sem=send_sem.at[flow, q, p], recv_sem=recv_sem.at[flow, q, p],
            device_id={"fsdp": me + 1 - 2 * flow}, device_id_type=mesh_id,
        )

    def add(flow, q, p):
        at = pl.ds(p * PIECE, PIECE)
        d = flow * (n_fsdp - 1 - q) + (1 - flow) * q
        forward(flow, q, p).wait_recv()
        mine[d, :, at] += inbox[flow, d, :, at]

    near_list = [(q, p) for q in range(n_fsdp - 1, 0, -1) for p in range(pieces)]
    far_list = [(q, p) for q in range(n_fsdp - 1, n_fsdp // 2, -1) for p in range(pieces)]
    burst = max(pieces, min(BURST, len(near_list)))

    loads[1].wait()
    pl.semaphore_wait(barrier, n_dp - 1 + n_fsdp - 1)
    for p in range(pieces):
        at = pl.ds(p * PIECE, PIECE)
        for layer in range(layers):
            x = grad[layer, :, at].astype(F32)
            for d in range(n_fsdp):
                mine[d, layer * own:(layer + 1) * own, at] = x[d * own:(d + 1) * own]

        @pl.when(near_pos == 0)
        def _():
            forward(near, *near_list[p]).start()

    @pl.when(near_pos == 0)
    def _():
        for q, p in near_list[pieces:burst]:
            forward(near, q, p).start()

    loads[0].wait()

    def by_index(shape, dim):
        j = lax.broadcasted_iota(jnp.int32, shape, dim) % KEEP
        k = jnp.zeros(shape, jnp.int32)
        for i in range(KEEP):
            k = jnp.where(j == i, kept_ref[i], k)
        return k

    row = cosine_rows(by_index((KEEP, lanes), 0), lax.broadcasted_iota(jnp.int32, (KEEP, lanes), 1) % SPAN)
    column = cosine_rows(by_index((SPAN, lanes), 1), lax.broadcasted_iota(jnp.int32, (SPAN, lanes), 0))
    lane_block = lax.broadcasted_iota(jnp.int32, (SPAN, lanes), 1) // KEEP
    coef = jnp.concatenate([jnp.where(lane_block == b, column, 0.0) for b in range(GROUP // SPAN)], axis=0)
    wide = jnp.concatenate([row] * (PIECE // lanes), axis=1)
    wide_block = lax.broadcasted_iota(jnp.int32, (KEEP, PIECE), 1) // SPAN
    back = jnp.concatenate([jnp.where(wide_block == b, wide, 0.0) for b in range(PIECE // SPAN)], axis=0)
    high, low = halves(coef)
    w_coef[:, :lanes] = high
    w_coef[:, lanes:] = low
    high, low = halves(back)
    w_back[:lanes] = high
    w_back[lanes:] = low

    def first_copy(p):
        return pltpu.make_async_remote_copy(
            src_ref=own_coef.at[p], dst_ref=dp_parts.at[dp],
            send_sem=first_send.at[p], recv_sem=first_recv.at[dp],
            device_id={"dp": p}, device_id_type=mesh_id,
        )

    def first_arrival(source):
        return pltpu.make_async_remote_copy(
            src_ref=own_coef.at[0], dst_ref=dp_parts.at[source],
            send_sem=first_send.at[0], recv_sem=first_recv.at[source],
            device_id={"dp": source}, device_id_type=mesh_id,
        )

    def second_copy(i):
        target = lax.rem(me + i, n_fsdp)
        return pltpu.make_async_remote_copy(
            src_ref=dp_sum.at[target], dst_ref=fsdp_parts.at[me],
            send_sem=second_send.at[i], recv_sem=second_recv.at[me],
            device_id={"fsdp": target}, device_id_type=mesh_id,
        )

    def second_arrival(source):
        return pltpu.make_async_remote_copy(
            src_ref=dp_sum.at[0], dst_ref=fsdp_parts.at[source],
            send_sem=second_send.at[0], recv_sem=second_recv.at[source],
            device_id={"fsdp": source}, device_id_type=mesh_id,
        )

    def third_copy(i):
        return pltpu.make_async_remote_copy(
            src_ref=total.at[dp], dst_ref=total.at[dp],
            send_sem=third_send.at[i], recv_sem=third_recv.at[dp],
            device_id={"dp": lax.rem(dp + i, n_dp)}, device_id_type=mesh_id,
        )

    def third_arrival(p):
        return pltpu.make_async_remote_copy(
            src_ref=total.at[p], dst_ref=total.at[p],
            send_sem=third_send.at[0], recv_sem=third_recv.at[p],
            device_id={"dp": p}, device_id_type=mesh_id,
        )

    def pack(out, height):
        packed = out[:height]
        for q in range(1, parts):
            packed += pltpu.roll(out[q * height:(q + 1) * height], q * (lanes // parts), 1)
        return packed

    def state(p):
        at = pl.ds(p * PIECE, PIECE)
        return 0.9 * jnp.concatenate([mom[layer, :, at] for layer in range(layers)], axis=0)

    def stacked(x):
        return jnp.concatenate([x[:, q * GROUP:(q + 1) * GROUP] for q in range(parts)], axis=0)

    loads[2].wait()
    for p in range(pieces):
        tall = [stacked(grad[layer, :, pl.ds(p * PIECE, PIECE)]) for layer in range(layers)]
        tall += list(halves(stacked(state(p))))
        out = dot(jnp.concatenate(tall, axis=0), w_coef[...])
        out = out[:, :lanes] + out[:, lanes:]
        step = parts * rows
        for layer in range(layers):
            packed = pack(out[layer * step:(layer + 1) * step], rows)
            for d in range(n_fsdp):
                own_coef[p, d, layer * own:(layer + 1) * own] = packed[d * own:(d + 1) * own]
        out = out[layers * step:]
        height = layers * own
        own_coef[p, me] += pack(out[:parts * height] + out[parts * height:], height)

        @pl.when(dp != p)
        def _():
            first_copy(p).start()

    proj = jnp.dot(coef, back[:, :GROUP], precision=lax.Precision.HIGHEST, preferred_element_type=F32)
    high, low = halves(proj)
    w_proj[:, :GROUP] = high
    w_proj[:, GROUP:] = low

    def sum_dp():
        @pl.when(dp < pieces)
        def _():
            dp_parts[dp] = own_coef[dp]
            for i in range(1, n_dp):
                first_arrival(lax.rem(dp + i, n_dp)).wait_recv()
            for d in range(n_fsdp):
                value = dp_parts[0, d]
                for r in range(1, n_dp):
                    value += dp_parts[r, d]
                dp_sum[d] = value
            for i in range(1, n_fsdp):
                second_copy(i).start()

    def sum_fsdp():
        @pl.when(dp < pieces)
        def _():
            fsdp_parts[me] = dp_sum[me]
            for i in range(1, n_fsdp):
                second_arrival(lax.rem(me + i, n_fsdp)).wait_recv()
            value = fsdp_parts[0]
            for f in range(1, n_fsdp):
                value += fsdp_parts[f]
            total[dp] = value
            for i in range(1, n_dp):
                third_copy(i).start()

    def update_params():
        for p in range(pieces):
            @pl.when(dp != p)
            def _():
                third_arrival(p).wait_recv()
        shared = jnp.concatenate([total[p] for p in range(pieces)], axis=0) / n_dp
        high, low = halves(shared)
        left = jnp.concatenate([high, low], axis=0)
        right = jnp.concatenate([high, jnp.zeros_like(low)], axis=0)
        out = dot(jnp.concatenate([left, right], axis=1), w_back[...])
        half = shared.shape[0]
        update = out[:half] + out[half:]
        height = layers * own
        loads[3].wait()
        for p in range(pieces):
            at = pl.ds(p * PIECE, PIECE)
            for layer in range(layers):
                top = p * height + layer * own
                new_par[layer, :, at] = par[layer, :, at] - update[top:top + own]

    def near_step(i):
        q, p = near_list[i]

        if q > 1:
            @pl.when((near_pos > 0) & (near_pos < q))
            def _():
                add(near, q, p)
                forward(near, q, p).start()

    def far_step(q, p):
        @pl.when(far_pos < q)
        def _():
            add(far, q, p)
            forward(far, q, p).start()

    @pl.when(near_pos == 0)
    def _():
        sum_dp()
        for q, p in near_list[burst:]:
            forward(near, q, p).start()
        sum_fsdp()

    for i in range(len(near_list)):
        near_step(i)
        if 0 <= i - LAG < len(far_list):
            far_step(*far_list[i - LAG])
        if i == min(SUM_DP, len(near_list) - 1):
            pl.when(near_pos > 0)(sum_dp)
        if i == min(SUM_FSDP, len(near_list) - 1):
            pl.when(near_pos > 0)(sum_fsdp)

    def finish_sends():
        for q, p in near_list:
            @pl.when((near_pos > 0) & (near_pos < q))
            def _():
                forward(near, q, p).wait_send()
        for q, p in far_list:
            @pl.when(far_pos < q)
            def _():
                forward(far, q, p).wait_send()
        for p in range(pieces):
            @pl.when(dp != p)
            def _():
                first_copy(p).wait_send()

        @pl.when(dp < pieces)
        def _():
            for i in range(1, n_fsdp):
                second_copy(i).wait_send()
            for i in range(1, n_dp):
                third_copy(i).wait_send()

    height = layers * own
    groups = [range(p, min(p + 2, pieces)) for p in range(0, pieces, 2)]
    for g, group in enumerate(groups):
        if g == min(1, len(groups) - 1):
            update_params()
        if g == len(groups) - 1:
            finish_sends()
        tall = []
        for p in group:
            add(far, far_pos, p)

            @pl.when(near_pos > 0)
            def _():
                add(near, near_pos, p)

            tall.append(stacked(state(p) + mine[me, :, pl.ds(p * PIECE, PIECE)]))
        tall = jnp.concatenate(tall, axis=0)
        half = tall.shape[0]
        out = dot(jnp.concatenate(halves(tall), axis=0), w_proj[...])
        rest = tall - (out[:half, :GROUP] + (out[half:, :GROUP] + out[:half, GROUP:]))
        for j in range(len(group) * parts):
            at = pl.ds(group[0] * PIECE + j * GROUP, GROUP)
            for layer in range(layers):
                new_mom[layer, :, at] = rest[j * height + layer * own:j * height + (layer + 1) * own]

    @pl.when(near_pos == 0)
    def _():
        for q, p in near_list:
            forward(near, q, p).wait_send()


def store(new_par, new_mom, new_par_hbm, new_mom_hbm, sem):
    copies = [
        pltpu.make_async_copy(new_par, new_par_hbm, sem.at[0]),
        pltpu.make_async_copy(new_mom, new_mom_hbm.at[0], sem.at[1]),
    ]
    for copy in copies:
        copy.start()
    for copy in copies:
        copy.wait()


def shards(n_dp, n_fsdp, grad_partials, momentum, params, kept):
    _, _, layers, rows, cols = grad_partials.shape
    own = rows // n_fsdp
    pieces = cols // PIECE
    held = (layers, own, cols)
    tile = (layers * own, 128)
    chunk = (n_fsdp, layers * own, cols)
    anywhere = pl.BlockSpec(memory_space=pl.ANY)
    vmem = pl.BlockSpec(memory_space=pltpu.VMEM)
    inputs = [pltpu.with_memory_space_constraint(x, pltpu.HBM) for x in (grad_partials, momentum, params, kept)]
    sem = pltpu.SemaphoreType.DMA
    results = pl.pallas_call(
        functools.partial(kernel, n_dp, n_fsdp),
        out_shape=(pltpu.VMEM(held, F32), pltpu.VMEM(held, F32)),
        in_specs=[anywhere, anywhere, anywhere, anywhere],
        out_specs=(vmem, vmem),
        scratch_shapes=[
            pltpu.SMEM((KEEP,), jnp.int32),
            pltpu.VMEM((layers, rows, cols), BF16),
            pltpu.VMEM(held, F32),
            pltpu.VMEM(held, F32),
            pltpu.VMEM(chunk, F32),
            pltpu.VMEM((2,) + chunk, F32),
            pltpu.VMEM((pieces, n_fsdp) + tile, F32),
            pltpu.VMEM((n_dp, n_fsdp) + tile, F32),
            pltpu.VMEM((n_fsdp,) + tile, F32),
            pltpu.VMEM((n_fsdp,) + tile, F32),
            pltpu.VMEM((pieces,) + tile, F32),
            pltpu.VMEM((GROUP, 256), BF16),
            pltpu.VMEM((GROUP, 2 * GROUP), BF16),
            pltpu.VMEM((256, PIECE), BF16),
            sem((4,)),
            sem((2, n_fsdp, pieces)),
            sem((2, n_fsdp, pieces)),
            sem((pieces,)),
            sem((n_dp,)),
            sem((n_fsdp,)),
            sem((n_fsdp,)),
            sem((n_dp,)),
            sem((pieces,)),
        ],
        compiler_params=pltpu.CompilerParams(
            collective_id=0, has_side_effects=True, vmem_limit_bytes=48 * 1024 * 1024
        ),
    )(*inputs)
    results = [pltpu.with_memory_space_constraint(x, pltpu.VMEM) for x in results]
    return pl.pallas_call(
        store,
        out_shape=(
            jax.ShapeDtypeStruct(params.shape, F32),
            jax.ShapeDtypeStruct(momentum.shape, F32),
        ),
        in_specs=[vmem, vmem],
        out_specs=(anywhere, anywhere),
        scratch_shapes=[sem((2,))],
        compiler_params=pltpu.CompilerParams(vmem_limit_bytes=60 * 1024 * 1024),
    )(*results)


def solution(mesh):
    placed = (
        P("dp", "fsdp", None, None, None),
        P("dp", None, "fsdp", None),
        P(None, "fsdp", None),
        P(),
    )
    return jax.shard_map(
        functools.partial(shards, mesh.shape["dp"], mesh.shape["fsdp"]),
        mesh=mesh,
        in_specs=placed,
        out_specs=(P(None, "fsdp", None), P("dp", None, "fsdp", None)),
        check_vma=False,
    )
```
